32 devices in a mesh: groups: 2 (over y), req: 8 (over z, x), tp: 2 (over core).
Axes of the slice: x: 2, y: 2, z: 4, core: 2. Of those that a mesh axis runs over, the one named last changes fastest.
Arguments:
- projected_queries: bfloat16 [4096, 8192], P(('groups', 'req'), 'tp'), parts along dimension 0, may hold values from -6 to 6
- projected_keys: bfloat16 [4096, 1024], P(('groups', 'req'), 'tp'), parts along dimension 0, may hold values from -6 to 6
- projected_values: bfloat16 [4096, 1024], P(('groups', 'req'), 'tp'), parts along dimension 0, may hold values from -6 to 6
- request_adapter: int32 [8], P('groups'), parts along dimension 0, may hold values from 0 to 7
- adapter_slot_table: int32 [16], P('groups'), parts along dimension 0, may hold values from 0 to 7, each once
- adapter_down_factor: bfloat16 [16, 64, 128, 64], P(('groups', 'req'), 'tp'), parts along dimension 0, may hold values from -0.0625 to 0.0625
- adapter_up_factor: bfloat16 [16, 64, 40, 128], P(('groups', 'req'), None, 'tp'), parts along dimension 0, may hold values from -0.75 to 0.75
Outputs:
- adapter_delta: bfloat16 [4096, 5120], P(('groups', 'req'), 'tp'), parts along dimension 0
The draws below stay inside these ranges and needn't reach their ends.
There are 2 independent parts, one for each index of `groups`. The reference program is written for one: setup_inputs(seed, part) draws one part's arguments, and reference() takes and returns one part's arrays. A program takes and returns all parts, laid end to end along the dimension named above; each array names one. Nothing has to cross between parts.
Inputs may be any that keep to these rules, and one draw needn't show every extreme that they name: `adapter_slot_table`: each slot once.
All inputs are finite; a program needn't handle non-finite values.
Results may differ from the reference program's by a relative error of at most 0.012.
Values may be sent and summed in bfloat16 or wider, within the bound.
No kernel may reach another device: no remote copies, remote signals or barrier semaphores. Data moves between devices by JAX's collectives and lax.ppermute only.
A program may use at most 64 MiB of HBM per device.

```python
import math
import jax
import jax.numpy as jnp
import numpy as np
from jax import lax

MODEL_WIDTH = 5120
QUERY_HEAD_COUNT = 64
KEY_VALUE_HEADS = 8
HEAD_SIZE = 128
ADAPTER_RANK = 64
TOK_DEV = 256
ADAPTER_COUNT = 8
REQUEST_COUNT = 4
TOKEN_COUNT = 2048


def draw_projected_keys(key, part):
    key = jax.random.fold_in(key, 3)
    return jnp.clip(jax.random.normal(key, (TOKEN_COUNT, KEY_VALUE_HEADS * HEAD_SIZE), jnp.float32), -6.0, 6.0).astype(jnp.bfloat16)


def draw_projected_queries(key, part):
    key = jax.random.fold_in(key, 5)
    return jnp.clip(jax.random.normal(key, (TOKEN_COUNT, QUERY_HEAD_COUNT * HEAD_SIZE), jnp.float32), -6.0, 6.0).astype(jnp.bfloat16)


def touch_ends(drawn, stream_key, low, top_value):
    index_at = [jax.random.randint(jax.random.fold_in(stream_key, axis), (), 0, length) for axis, length in enumerate(drawn.shape)]
    widest = drawn.shape.index(max(drawn.shape))
    next_to = index_at[:widest] + [(index_at[widest] + 1) % drawn.shape[widest]] + index_at[widest + 1:]
    return drawn.at[tuple(index_at)].set(low).at[tuple(next_to)].set(top_value)


def levels(rng, extent, split, smallest, largest):
    level, own = 1.0, jax.random.fold_in(rng, 6)
    for dim, blocks in split:
        steps = jnp.exp(jax.random.uniform(jax.random.fold_in(own, dim), (blocks,), jnp.float32, smallest / len(split), largest / len(split)))
        level = level * jnp.repeat(steps, extent[dim] // blocks).reshape([-1 if axis == dim else 1 for axis in range(len(extent))])
    return level


def rank_bounds(number_of, lean):
    loads = [(1 << 20) // math.isqrt(rank ** lean) + 1 for rank in range(1, number_of + 1)]
    scale = 1 + sum(loads) // (1 << 30)
    return np.cumsum(np.array([max(1, weight // scale) for weight in loads]))


def ranked(own_key, shape, amount, lean):
    grid = rank_bounds(amount, lean)
    ticket = jax.random.randint(jax.random.fold_in(own_key, 1), shape, 0, int(grid[amount - 1]))
    grade = jnp.searchsorted(jnp.asarray(grid, jnp.int32), ticket, side="right")
    return jax.random.permutation(jax.random.fold_in(own_key, 2), amount)[grade].astype(jnp.int32)


def scatter_about(stream_key, shape, width, limit, pieces=(), dtype=jnp.bfloat16):
    entries = jax.random.normal(stream_key, shape, jnp.float32) * width
    if len(pieces) > 0:
        entries = levels(stream_key, shape, pieces, -0.22, 0.18) * entries
    return jnp.clip(entries, min=-limit, max=limit).astype(dtype)


def setup_inputs(seed: int = 0, part: int = 0) -> dict:
    seeds = jax.random.split(jax.random.key(seed), 8)
    part_keys = jax.random.split(jax.random.fold_in(seeds[7], part), 8)
    return {
        "projected_queries": draw_projected_queries(jax.random.fold_in(jax.random.fold_in(seeds[7], part), 71), part),
        "projected_keys": draw_projected_keys(jax.random.fold_in(jax.random.fold_in(seeds[7], part), 71), part),
        "projected_values": scatter_about(part_keys[2], (TOKEN_COUNT, KEY_VALUE_HEADS * HEAD_SIZE), 1.0, 6.0, ((0, 8), (1, 2))),
        "request_adapter": touch_ends(ranked(part_keys[3], (REQUEST_COUNT,), ADAPTER_COUNT, 2), jax.random.fold_in(part_keys[3], 3), 0, ADAPTER_COUNT - 1).astype(jnp.int32),
        "adapter_slot_table": jax.random.permutation(part_keys[4], ADAPTER_COUNT).astype(jnp.int32),
        "adapter_down_factor": scatter_about(part_keys[5], (ADAPTER_COUNT, QUERY_HEAD_COUNT, HEAD_SIZE, ADAPTER_RANK), (QUERY_HEAD_COUNT * HEAD_SIZE) ** -0.5, 0.0625, ((0, 8), (1, 2))),
        "adapter_up_factor": scatter_about(part_keys[6], (ADAPTER_COUNT, ADAPTER_RANK, MODEL_WIDTH // 128, 128), ADAPTER_RANK ** -0.5, 0.75, ((0, 8), (2, 2))),
    }


def attend_request(query_request, key_request, value_request):
    request_length = query_request.shape[0]
    query_group_size = QUERY_HEAD_COUNT // KEY_VALUE_HEADS
    query_head_split = jnp.moveaxis(query_request.reshape(request_length, KEY_VALUE_HEADS, query_group_size, HEAD_SIZE), 1, 0).astype(jnp.float32)
    key_head_split = jnp.moveaxis(key_request.reshape(request_length, KEY_VALUE_HEADS, HEAD_SIZE), 1, 0).astype(jnp.float32)
    value_head_split = jnp.moveaxis(value_request.reshape(request_length, KEY_VALUE_HEADS, HEAD_SIZE), 1, 0).astype(jnp.float32)
    positions = jnp.arange(request_length)
    visible = positions[None, :] <= positions[:, None]
    score_scale = 1.0 / math.sqrt(HEAD_SIZE)

    def per_head(head_data):
        query_head, key_head, value_head = head_data
        scores = jnp.einsum('tgd,sd->tgs', query_head, key_head) * score_scale
        scores = jnp.where(visible[:, None, :], scores, -1e+30)
        row_peak = lax.optimization_barrier(jnp.max(scores, axis=2, keepdims=True))
        exp_terms = jnp.where(visible[:, None, :], jnp.exp(scores - row_peak), 0.0)
        row_total = lax.optimization_barrier(jnp.sum(exp_terms, axis=2))
        weights = lax.optimization_barrier(exp_terms.astype(jnp.bfloat16))
        head_out = jnp.einsum('tgs,sd->tgd', weights.astype(jnp.float32), value_head)
        return head_out / row_total[..., None]
    outputs = lax.map(per_head, (query_head_split, key_head_split, value_head_split))
    return jnp.moveaxis(outputs, 0, 1).reshape(request_length, QUERY_HEAD_COUNT * HEAD_SIZE)

def reference(projected_queries, projected_keys, projected_values, request_adapter, adapter_slot_table, adapter_down_factor, adapter_up_factor):
    request_length = 2 * TOK_DEV
    query_request = projected_queries.reshape(REQUEST_COUNT, request_length, QUERY_HEAD_COUNT * HEAD_SIZE)
    key_request = projected_keys.reshape(REQUEST_COUNT, request_length, KEY_VALUE_HEADS * HEAD_SIZE)
    value_request = projected_values.reshape(REQUEST_COUNT, request_length, KEY_VALUE_HEADS * HEAD_SIZE)

    def per_request(request_data):
        query_one, key_one, value_one, adapter = request_data
        context = attend_request(query_one, key_one, value_one).astype(jnp.bfloat16)
        library_slot_index = adapter_slot_table[adapter].astype(jnp.int32)
        down_factor_panel = lax.dynamic_index_in_dim(adapter_down_factor, library_slot_index, 0, keepdims=False).reshape(QUERY_HEAD_COUNT * HEAD_SIZE, ADAPTER_RANK)
        up_factor_panel = lax.dynamic_index_in_dim(adapter_up_factor, library_slot_index, 0, keepdims=False).reshape(ADAPTER_RANK, MODEL_WIDTH)
        rank_mix = jnp.dot(context, down_factor_panel, preferred_element_type=jnp.float32).astype(jnp.bfloat16)
        return (2.0 * jnp.dot(rank_mix, up_factor_panel, preferred_element_type=jnp.float32)).astype(jnp.bfloat16)
    results = lax.map(per_request, (query_request, key_request, value_request, request_adapter.astype(jnp.int32)))
    return results.reshape(TOKEN_COUNT, MODEL_WIDTH)
```

```python
import functools
import math

import jax
import jax.numpy as jnp
from jax import lax
from jax.experimental import pallas as pl
from jax.experimental.pallas import tpu as pltpu
from jax.sharding import PartitionSpec as P

QUERY_HEAD_COUNT = 64
KEY_VALUE_HEADS = 8
HEAD_SIZE = 128
ADAPTER_RANK = 64
GROUP = QUERY_HEAD_COUNT // KEY_VALUE_HEADS
EXP2_SCALE = math.log2(math.e) / math.sqrt(HEAD_SIZE)
VMEM_LIMIT = 32 << 20
MINOR_BOTH = (((1,), (1,)), ((), ()))
PLAIN = (((1,), (0,)), ((), ()))


def dot(lhs, rhs, dims=PLAIN):
    return lax.dot_general(lhs, rhs, dims, preferred_element_type=jnp.float32)


def swapped(shard, axis, mask):
    size = lax.axis_size(axis)
    return lax.ppermute(shard, axis, [(i, i ^ mask) for i in range(size)])


def attend_kernel(parity_ref, query_ref, key_ref, value_ref, far_key_ref, far_value_ref, context_ref):
    rows = key_ref.shape[0]
    ones = jnp.ones((rows, HEAD_SIZE), jnp.bfloat16)
    causal = lax.broadcasted_iota(jnp.int32, (rows, rows), 0) >= lax.broadcasted_iota(
        jnp.int32, (rows, rows), 1
    )

    def run(with_far):
        near_key = key_ref[...]
        near_value = jnp.concatenate([value_ref[...], ones], axis=1)
        if with_far:
            far_key = far_key_ref[...]
            far_value = jnp.concatenate([far_value_ref[...], ones], axis=1)
        for head in range(GROUP):
            columns = slice(head * HEAD_SIZE, (head + 1) * HEAD_SIZE)
            query = query_ref[:, columns]
            near = jnp.where(causal, dot(query, near_key, MINOR_BOTH), -1e30)
            peak = jnp.max(near, axis=1, keepdims=True)
            if with_far:
                far = dot(query, far_key, MINOR_BOTH)
                peak = jnp.maximum(peak, jnp.max(far, axis=1, keepdims=True))
            out = dot(jnp.exp2((near - peak) * EXP2_SCALE).astype(jnp.bfloat16), near_value)
            if with_far:
                out += dot(jnp.exp2((far - peak) * EXP2_SCALE).astype(jnp.bfloat16), far_value)
            context_ref[0, :, columns] = (out[:, :HEAD_SIZE] / out[:, HEAD_SIZE:]).astype(jnp.bfloat16)

    @pl.when(parity_ref[0] == 0)
    def _():
        run(False)

    @pl.when(parity_ref[0] != 0)
    def _():
        run(True)


def attend(parity, queries, keys, values, far_keys, far_values):
    rows, width = queries.shape
    kv_count = keys.shape[1] // HEAD_SIZE
    kv_spec = pl.BlockSpec((rows, HEAD_SIZE), lambda g: (0, g))
    pairs = 2 * rows * rows * width
    return pl.pallas_call(
        attend_kernel,
        grid=(kv_count,),
        in_specs=[
            pl.BlockSpec(memory_space=pltpu.SMEM),
            pl.BlockSpec((rows, GROUP * HEAD_SIZE), lambda g: (0, g)),
            kv_spec,
            kv_spec,
            kv_spec,
            kv_spec,
        ],
        out_specs=pl.BlockSpec((1, rows, GROUP * HEAD_SIZE), lambda g: (g, 0, 0)),
        out_shape=jax.ShapeDtypeStruct((kv_count, rows, GROUP * HEAD_SIZE), jnp.bfloat16),
        compiler_params=pltpu.CompilerParams(vmem_limit_bytes=VMEM_LIMIT),
        cost_estimate=pl.CostEstimate(
            flops=6 * pairs, bytes_accessed=4 * rows * width, transcendentals=pairs // HEAD_SIZE
        ),
        name="attend",
    )(parity, queries, keys, values, far_keys, far_values)


def rank_kernel(quarter_ref, context_ref, held_ref, got_ref, rank_ref):
    total = jnp.zeros(rank_ref.shape, jnp.float32)
    for part in range(4):
        panel_ref = held_ref if part < 2 else got_ref
        quarter = quarter_ref[part]
        for head in range(0, GROUP, 2):
            context = context_ref[quarter, :, head * HEAD_SIZE : (head + 2) * HEAD_SIZE]
            panel = jnp.concatenate(
                [panel_ref[part % 2, head], panel_ref[part % 2, head + 1]], axis=1
            )
            total += dot(context, panel, MINOR_BOTH)
    rank_ref[...] = total


def rank_of(quarters, context, held, got):
    rows = context.shape[1]
    whole = pl.BlockSpec(memory_space=pltpu.VMEM)
    return pl.pallas_call(
        rank_kernel,
        in_specs=[pl.BlockSpec(memory_space=pltpu.SMEM), whole, whole, whole],
        out_specs=whole,
        out_shape=jax.ShapeDtypeStruct((rows, ADAPTER_RANK), jnp.float32),
        compiler_params=pltpu.CompilerParams(vmem_limit_bytes=VMEM_LIMIT),
        name="rank_mix",
    )(quarters, context, held, got)


def delta_kernel(quarter_ref, near_ref, far_ref, held_ref, got_ref, out_ref):
    step = pl.program_id(0)
    rank = (near_ref[...] + far_ref[...]).astype(jnp.bfloat16)

    def emit(panel_ref):
        for at in range(2):

            @pl.when(step % 2 == at)
            def _():
                panel = jnp.concatenate([panel_ref[at, b] for b in range(panel_ref.shape[1])], axis=1)
                out_ref[...] = (2.0 * dot(rank, panel)).astype(jnp.bfloat16)

    @pl.when(step < 2)
    def _():
        emit(held_ref)

    @pl.when(step >= 2)
    def _():
        emit(got_ref)


def delta_of(quarters, near, far, held, got):
    rows = near.shape[0]
    wide = held.shape[1] * held.shape[3]
    whole = lambda shape: pl.BlockSpec(shape, lambda s, q: (0,) * len(shape))
    return pl.pallas_call(
        delta_kernel,
        grid_spec=pltpu.PrefetchScalarGridSpec(
            num_scalar_prefetch=1,
            grid=(4,),
            in_specs=[whole(near.shape), whole(far.shape), whole(held.shape), whole(got.shape)],
            out_specs=pl.BlockSpec((rows, wide), lambda s, q: (0, q[s])),
        ),
        out_shape=jax.ShapeDtypeStruct((rows, 4 * wide), jnp.bfloat16),
        compiler_params=pltpu.CompilerParams(vmem_limit_bytes=VMEM_LIMIT),
        name="delta",
    )(quarters, near, far, held, got)


def pick(index, cases):
    return lax.select_n(index.astype(jnp.int32), *cases)


def spread(blocks, me):
    count = blocks.shape[0] // 4
    cut = lambda quarter: lax.dynamic_slice_in_dim(blocks, quarter * count, count, 0)
    return [cut(me % 4)] + [swapped(cut((me ^ k) % 4), "req", k) for k in (1, 2, 3)]


def deliver(quarters, me, slots):
    chosen = lambda request: pick((slots[request] ^ me) & 3, quarters)
    request = me // 2
    near = chosen(request)
    came = [swapped(chosen(request ^ j), "req", 2 * j) for j in (1, 2, 3)]
    at_home = slots[request] // 4 == me // 4
    return jnp.stack([jnp.where(at_home, near, came[1]), jnp.where(at_home, came[0], came[2])])


def eight_way(context, me, down, up, slots):
    down_quarters = spread(down, me)
    up_quarters = spread(up, me)
    down_held = deliver(down_quarters, me, slots)
    up_held = deliver(up_quarters, me, slots)
    down_got = swapped(down_held, "req", 1)
    up_got = swapped(up_held, "req", 1)
    quarters = (me % 4) ^ jnp.array([0, 2, 1, 3], jnp.int32)
    rank = rank_of(quarters, context, down_held, down_got)
    return delta_of(quarters, rank, swapped(rank, "tp", 1), up_held, up_got)


def any_way(context, me, down, up, slots):
    partner_count = lax.axis_size("req")
    rows = context.shape[1]

    def exchanged(blocks):
        slot_count, block_count = blocks.shape[:2]
        tail = blocks.shape[2] // partner_count
        cut = blocks.reshape(slot_count, block_count, partner_count, tail, blocks.shape[3])
        cut = jnp.moveaxis(cut, 2, 1)
        library = lax.all_to_all(cut, "req", split_axis=1, concat_axis=0, tiled=True)[:, 0]
        wanted = jnp.take(library, slots[jnp.arange(partner_count) // 2], axis=0)
        return lax.all_to_all(wanted, "req", split_axis=0, concat_axis=0, tiled=True)

    down_all = exchanged(jnp.swapaxes(down, 2, 3))
    up_all = exchanged(jnp.swapaxes(up, 2, 3))
    flat = jnp.swapaxes(context, 0, 1).reshape(rows, down_all.shape[1], partner_count, down_all.shape[2])
    rank = jnp.einsum("thrp,rhpk->tk", flat, down_all, preferred_element_type=jnp.float32)
    rank = lax.psum(rank, "tp").astype(jnp.bfloat16)
    mixed = jnp.einsum("tk,rblk->tbrl", rank, up_all, preferred_element_type=jnp.float32)
    return (2.0 * mixed.reshape(rows, -1)).astype(jnp.bfloat16)


def body(
    projected_queries,
    projected_keys,
    projected_values,
    request_adapter,
    adapter_slot_table,
    adapter_down_factor,
    adapter_up_factor,
):
    me = lax.axis_index("req")
    far_keys = swapped(projected_keys, "req", 1)
    far_values = swapped(projected_values, "req", 1)
    context = attend(
        (me % 2).reshape(1), projected_queries, projected_keys, projected_values, far_keys, far_values
    )
    slots = adapter_slot_table[request_adapter]
    down = jnp.swapaxes(adapter_down_factor, 2, 3)
    up = jnp.swapaxes(adapter_up_factor, 1, 2)
    if lax.axis_size("req") == 8 and down.shape[0] == 1:
        return eight_way(context, me, down[0], up[0], slots)
    return any_way(context, me, down, up, slots)


def solution(mesh):
    placed = (
        P(("groups", "req"), "tp"),
        P(("groups", "req"), "tp"),
        P(("groups", "req"), "tp"),
        P("groups"),
        P("groups"),
        P(("groups", "req"), "tp", None, None),
        P(("groups", "req"), None, "tp", None),
    )
    return jax.shard_map(
        body, mesh=mesh, in_specs=placed, out_specs=P(("groups", "req"), "tp"), check_vma=False
    )
```

```python
import functools
import math

import jax
import jax.numpy as jnp
from jax import lax
from jax.experimental import pallas as pl
from jax.experimental.pallas import tpu as pltpu
from jax.sharding import PartitionSpec as P

QUERY_HEAD_COUNT = 64
KEY_VALUE_HEADS = 8
HEAD_SIZE = 128
ADAPTER_RANK = 64
GROUP = QUERY_HEAD_COUNT // KEY_VALUE_HEADS
EXP2_SCALE = math.log2(math.e) / math.sqrt(HEAD_SIZE)
VMEM_LIMIT = 32 << 20
MINOR_BOTH = (((1,), (1,)), ((), ()))
PLAIN = (((1,), (0,)), ((), ()))


def dot(lhs, rhs, dims=PLAIN):
    return lax.dot_general(lhs, rhs, dims, preferred_element_type=jnp.float32)


def swapped(shard, axis, mask):
    size = lax.axis_size(axis)
    return lax.ppermute(shard, axis, [(i, i ^ mask) for i in range(size)])


def attend_kernel(query_ref, key_ref, value_ref, far_key_ref, far_value_ref, context_ref):
    rows = key_ref.shape[0]
    ones = jnp.ones((rows, HEAD_SIZE), jnp.bfloat16)
    causal = lax.broadcasted_iota(jnp.int32, (rows, rows), 0) >= lax.broadcasted_iota(
        jnp.int32, (rows, rows), 1
    )

    def run(with_far):
        near_key = key_ref[...]
        near_value = jnp.concatenate([value_ref[...], ones], axis=1)
        if with_far:
            far_key = far_key_ref[...]
            far_value = jnp.concatenate([far_value_ref[...], ones], axis=1)
        for head in range(GROUP):
            columns = slice(head * HEAD_SIZE, (head + 1) * HEAD_SIZE)
            query = query_ref[:, columns]
            near = jnp.where(causal, dot(query, near_key, MINOR_BOTH), -1e30)
            peak = jnp.max(near, axis=1, keepdims=True)
            if with_far:
                far = dot(query, far_key, MINOR_BOTH)
                peak = jnp.maximum(peak, jnp.max(far, axis=1, keepdims=True))
            out = dot(jnp.exp2((near - peak) * EXP2_SCALE).astype(jnp.bfloat16), near_value)
            if with_far:
                out += dot(jnp.exp2((far - peak) * EXP2_SCALE).astype(jnp.bfloat16), far_value)
            context_ref[0, :, columns] = (out[:, :HEAD_SIZE] / out[:, HEAD_SIZE:]).astype(jnp.bfloat16)

    parity = lax.axis_index("req") & 1

    @pl.when(parity == 0)
    def _():
        run(False)

    @pl.when(parity != 0)
    def _():
        run(True)


def attend(queries, keys, values, far_keys, far_values):
    rows, width = queries.shape
    kv_count = keys.shape[1] // HEAD_SIZE
    kv_spec = pl.BlockSpec((rows, HEAD_SIZE), lambda g: (0, g))
    pairs = 2 * rows * rows * width
    return pl.pallas_call(
        attend_kernel,
        grid=(kv_count,),
        in_specs=[
            pl.BlockSpec((rows, GROUP * HEAD_SIZE), lambda g: (0, g)),
            kv_spec,
            kv_spec,
            kv_spec,
            kv_spec,
        ],
        out_specs=pl.BlockSpec((1, rows, GROUP * HEAD_SIZE), lambda g: (g, 0, 0)),
        out_shape=jax.ShapeDtypeStruct((kv_count, rows, GROUP * HEAD_SIZE), jnp.bfloat16),
        compiler_params=pltpu.CompilerParams(vmem_limit_bytes=VMEM_LIMIT),
        cost_estimate=pl.CostEstimate(
            flops=6 * pairs, bytes_accessed=4 * rows * width, transcendentals=pairs // HEAD_SIZE
        ),
        name="attend",
    )(queries, keys, values, far_keys, far_values)


def in_vmem(kernel, name, out_shape, index_args, *arrays):
    return pl.pallas_call(
        kernel,
        in_specs=[pl.BlockSpec(memory_space=pltpu.SMEM)] * len(index_args)
        + [pl.BlockSpec(memory_space=pltpu.VMEM)] * len(arrays),
        out_specs=jax.tree.map(lambda _: pl.BlockSpec(memory_space=pltpu.VMEM), out_shape),
        out_shape=out_shape,
        compiler_params=pltpu.CompilerParams(vmem_limit_bytes=VMEM_LIMIT),
        name=name,
    )(*index_args, *arrays)


def slot_of(request, adapter_ref, table_ref):
    return table_ref[adapter_ref[request]]


def choose_kernel(adapter_ref, table_ref, *refs):
    me = lax.axis_index("req")
    for out, out_ref in enumerate(refs[4:]):
        wanted = (slot_of((me >> 1) ^ out, adapter_ref, table_ref) ^ me) & 3
        for k in range(4):

            @pl.when(wanted == k)
            def _():
                out_ref[...] = refs[k][...]


def assemble_kernel(adapter_ref, table_ref, *refs):
    me = lax.axis_index("req")
    home = (slot_of(me >> 1, adapter_ref, table_ref) ^ me) < 4

    @pl.when(home)
    def _():
        refs[4][0] = refs[0][...]
        refs[4][1] = refs[1][...]

    @pl.when(jnp.logical_not(home))
    def _():
        refs[4][0] = refs[2][...]
        refs[4][1] = refs[3][...]


def rank_kernel(adapter_ref, table_ref, context_ref, held_ref, got_ref, rank_ref):
    me = lax.axis_index("req")
    first = (slot_of(me >> 1, adapter_ref, table_ref) ^ me) & 3
    total = jnp.zeros(rank_ref.shape, jnp.float32)
    for part, bits in enumerate((0, 2, 1, 3)):
        panel_ref = held_ref if part < 2 else got_ref
        for head in range(0, GROUP, 2):
            context = context_ref[first ^ bits, :, head * HEAD_SIZE : (head + 2) * HEAD_SIZE]
            panel = jnp.concatenate(
                [panel_ref[part % 2, head], panel_ref[part % 2, head + 1]], axis=1
            )
            total += dot(context, panel, MINOR_BOTH)
    rank_ref[...] = total


def delta_kernel(adapter_ref, table_ref, near_ref, far_ref, held_ref, got_ref, out_ref, stage_ref, sems):
    me = lax.axis_index("req")
    first = (slot_of(me >> 1, adapter_ref, table_ref) ^ me) & 3
    rank = (near_ref[...] + far_ref[...]).astype(jnp.bfloat16)
    wide = stage_ref.shape[2]
    copies = []
    for part, bits in enumerate((0, 2, 1, 3)):
        panel_ref = held_ref if part < 2 else got_ref
        panel = jnp.concatenate(
            [panel_ref[part % 2, b] for b in range(panel_ref.shape[1])], axis=1
        )
        stage_ref[part] = (2.0 * dot(rank, panel)).astype(jnp.bfloat16)
        columns = pl.ds(pl.multiple_of((first ^ bits) * wide, HEAD_SIZE), wide)
        copy = pltpu.make_async_copy(stage_ref.at[part], out_ref.at[:, columns], sems.at[part])
        copy.start()
        copies.append(copy)
    for copy in copies:
        copy.wait()


def delta_of(index_args, near, far, held, got):
    rows = near.shape[0]
    wide = held.shape[1] * held.shape[3]
    return pl.pallas_call(
        delta_kernel,
        in_specs=[pl.BlockSpec(memory_space=pltpu.SMEM)] * 2
        + [pl.BlockSpec(memory_space=pltpu.VMEM)] * 4,
        out_specs=pl.BlockSpec(memory_space=pl.ANY),
        out_shape=jax.ShapeDtypeStruct((rows, 4 * wide), jnp.bfloat16),
        scratch_shapes=[pltpu.VMEM((4, rows, wide), jnp.bfloat16), pltpu.SemaphoreType.DMA((4,))],
        compiler_params=pltpu.CompilerParams(vmem_limit_bytes=VMEM_LIMIT),
        name="delta",
    )(*index_args, near, far, held, got)


def spread(blocks):
    count = blocks.shape[0] // 4
    cut = [blocks[k * count : (k + 1) * count] for k in range(4)]
    return cut[:1] + [swapped(cut[k], "req", k) for k in (1, 2, 3)]


def deliver(index_args, quarters):
    shape = jax.ShapeDtypeStruct(quarters[0].shape, quarters[0].dtype)
    near, *sent = in_vmem(choose_kernel, "choose", [shape] * 4, index_args, *quarters)
    came = [swapped(panel, "req", 2 * j) for j, panel in enumerate(sent, 1)]
    both = jax.ShapeDtypeStruct((2, *shape.shape), shape.dtype)
    return in_vmem(assemble_kernel, "assemble", both, index_args, near, *came)


def eight_way(context, down, up, index_args):
    down_quarters = spread(down)
    up_quarters = spread(up)
    down_held = deliver(index_args, down_quarters)
    up_held = deliver(index_args, up_quarters)
    down_got = swapped(down_held, "req", 1)
    up_got = swapped(up_held, "req", 1)
    rank_shape = jax.ShapeDtypeStruct((context.shape[1], ADAPTER_RANK), jnp.float32)
    rank = in_vmem(rank_kernel, "rank_mix", rank_shape, index_args, context, down_held, down_got)
    return delta_of(index_args, rank, swapped(rank, "tp", 1), up_held, up_got)


def any_way(context, down, up, slots):
    partner_count = lax.axis_size("req")
    rows = context.shape[1]

    def exchanged(blocks):
        slot_count, block_count = blocks.shape[:2]
        tail = blocks.shape[2] // partner_count
        cut = blocks.reshape(slot_count, block_count, partner_count, tail, blocks.shape[3])
        cut = jnp.moveaxis(cut, 2, 1)
        library = lax.all_to_all(cut, "req", split_axis=1, concat_axis=0, tiled=True)[:, 0]
        wanted = jnp.take(library, slots[jnp.arange(partner_count) // 2], axis=0)
        return lax.all_to_all(wanted, "req", split_axis=0, concat_axis=0, tiled=True)

    down_all = exchanged(jnp.swapaxes(down, 2, 3))
    up_all = exchanged(jnp.swapaxes(up, 2, 3))
    flat = jnp.swapaxes(context, 0, 1).reshape(rows, down_all.shape[1], partner_count, down_all.shape[2])
    rank = jnp.einsum("thrp,rhpk->tk", flat, down_all, preferred_element_type=jnp.float32)
    rank = lax.psum(rank, "tp").astype(jnp.bfloat16)
    mixed = jnp.einsum("tk,rblk->tbrl", rank, up_all, preferred_element_type=jnp.float32)
    return (2.0 * mixed.reshape(rows, -1)).astype(jnp.bfloat16)


def body(
    projected_queries,
    projected_keys,
    projected_values,
    request_adapter,
    adapter_slot_table,
    adapter_down_factor,
    adapter_up_factor,
):
    far_keys = swapped(projected_keys, "req", 1)
    far_values = swapped(projected_values, "req", 1)
    context = attend(projected_queries, projected_keys, projected_values, far_keys, far_values)
    down = jnp.swapaxes(adapter_down_factor, 2, 3)
    up = jnp.swapaxes(adapter_up_factor, 1, 2)
    if lax.axis_size("req") == 8 and down.shape[0] == 1:
        return eight_way(context, down[0], up[0], (request_adapter, adapter_slot_table))
    return any_way(context, down, up, adapter_slot_table[request_adapter])


def solution(mesh):
    placed = (
        P(("groups", "req"), "tp"),
        P(("groups", "req"), "tp"),
        P(("groups", "req"), "tp"),
        P("groups"),
        P("groups"),
        P(("groups", "req"), "tp", None, None),
        P(("groups", "req"), None, "tp", None),
    )
    return jax.shard_map(
        body, mesh=mesh, in_specs=placed, out_specs=P(("groups", "req"), "tp"), check_vma=False
    )
```

```python
import functools
import math

import jax
import jax.numpy as jnp
from jax import lax
from jax.experimental import pallas as pl
from jax.experimental.pallas import tpu as pltpu
from jax.sharding import PartitionSpec as P

QUERY_HEAD_COUNT = 64
KEY_VALUE_HEADS = 8
HEAD_SIZE = 128
ADAPTER_RANK = 64
GROUP = QUERY_HEAD_COUNT // KEY_VALUE_HEADS
EXP2_SCALE = math.log2(math.e) / math.sqrt(HEAD_SIZE)
VMEM_LIMIT = 32 << 20
MINOR_BOTH = (((1,), (1,)), ((), ()))
PLAIN = (((1,), (0,)), ((), ()))


def dot(lhs, rhs, dims=PLAIN):
    return lax.dot_general(lhs, rhs, dims, preferred_element_type=jnp.float32)


def swapped(shard, axis, mask):
    size = lax.axis_size(axis)
    return lax.ppermute(shard, axis, [(i, i ^ mask) for i in range(size)])


def attend_kernel(query_ref, key_ref, value_ref, far_ref, context_ref):
    rows = key_ref.shape[0]
    ones = jnp.ones((rows, HEAD_SIZE), jnp.bfloat16)
    causal = lax.broadcasted_iota(jnp.int32, (rows, rows), 0) >= lax.broadcasted_iota(
        jnp.int32, (rows, rows), 1
    )

    def run(with_far):
        for group in range(context_ref.shape[0]):
            own = slice(group * HEAD_SIZE, (group + 1) * HEAD_SIZE)
            near_key = key_ref[:, own]
            near_value = jnp.concatenate([value_ref[:, own], ones], axis=1)
            if with_far:
                far_key = far_ref[:, own]
                far_value = jnp.concatenate([far_ref[:, key_ref.shape[1] + group * HEAD_SIZE : key_ref.shape[1] + (group + 1) * HEAD_SIZE], ones], axis=1)
            for head in range(GROUP):
                at = (group * GROUP + head) * HEAD_SIZE
                query = query_ref[:, at : at + HEAD_SIZE]
                near = jnp.where(causal, dot(query, near_key, MINOR_BOTH), -1e30)
                peak = jnp.max(near, axis=1, keepdims=True)
                if with_far:
                    far = dot(query, far_key, MINOR_BOTH)
                    peak = jnp.maximum(peak, jnp.max(far, axis=1, keepdims=True))
                out = dot(jnp.exp2((near - peak) * EXP2_SCALE).astype(jnp.bfloat16), near_value)
                if with_far:
                    out += dot(jnp.exp2((far - peak) * EXP2_SCALE).astype(jnp.bfloat16), far_value)
                context = (out[:, :HEAD_SIZE] / out[:, HEAD_SIZE:]).astype(jnp.bfloat16)
                context_ref[group, :, head * HEAD_SIZE : (head + 1) * HEAD_SIZE] = context

    parity = lax.axis_index("req") & 1

    @pl.when(parity == 0)
    def _():
        run(False)

    @pl.when(parity != 0)
    def _():
        run(True)


def attend(queries, keys, values, far):
    rows, width = queries.shape
    shape = (keys.shape[1] // HEAD_SIZE, rows, GROUP * HEAD_SIZE)
    whole = jax.ShapeDtypeStruct(shape, jnp.bfloat16)
    return in_vmem(attend_kernel, "attend", whole, None, queries, keys, values, far)


def in_vmem(kernel, name, out_shape, slots, *arrays, weight=0):
    scalars = [] if slots is None else [slots]
    return pl.pallas_call(
        kernel,
        in_specs=[pl.BlockSpec(memory_space=pltpu.SMEM)] * len(scalars)
        + [pl.BlockSpec(memory_space=pltpu.VMEM)] * len(arrays),
        out_specs=jax.tree.map(lambda _: pl.BlockSpec(memory_space=pltpu.VMEM), out_shape),
        out_shape=out_shape,
        compiler_params=pltpu.CompilerParams(vmem_limit_bytes=VMEM_LIMIT),
        cost_estimate=pl.CostEstimate(flops=weight, bytes_accessed=weight // 100, transcendentals=0),
        name=name,
    )(*scalars, *arrays)


def slots_kernel(adapter_ref, table_ref, slots_ref):
    for request in range(slots_ref.shape[0]):
        slots_ref[request] = table_ref[adapter_ref[request]]


def slots_of(request_adapter, adapter_slot_table):
    return pl.pallas_call(
        slots_kernel,
        in_specs=[pl.BlockSpec(memory_space=pltpu.SMEM)] * 2,
        out_specs=pl.BlockSpec(memory_space=pltpu.SMEM),
        out_shape=jax.ShapeDtypeStruct(request_adapter.shape, jnp.int32),
        cost_estimate=pl.CostEstimate(flops=0, bytes_accessed=0, transcendentals=0),
        name="slots",
    )(request_adapter, adapter_slot_table)


def take(request, me, slots_ref, quarter_refs, out_ref, at, other=None):
    where = slots_ref[request] ^ me
    for k in range(4):

        @pl.when((where if other is not None else where & 3) == k)
        def _():
            out_ref[at] = quarter_refs[k][...]

    if other is not None:

        @pl.when(where >= 4)
        def _():
            out_ref[at] = other[...]


def cross_kernel(slots_ref, *refs):
    me = lax.axis_index("req")
    for at in range(2):
        take((me >> 1) ^ (2 + at), me, slots_ref, refs[:4], refs[4], at)


def settle_kernel(slots_ref, *refs):
    me = lax.axis_index("req")
    for at in range(2):
        request = (me >> 1) ^ at
        take(request, me, slots_ref, refs[:4], refs[5 + at], ..., refs[4].at[at])


def rank_kernel(slots_ref, context_ref, *refs):
    me = lax.axis_index("req")
    first = (slots_ref[me >> 1] ^ me) & 3
    total = jnp.zeros(refs[4].shape, jnp.float32)
    for k in range(4):
        for head in range(0, GROUP, 2):
            context = context_ref[first ^ k, :, head * HEAD_SIZE : (head + 2) * HEAD_SIZE]
            panel = jnp.concatenate([refs[k][head], refs[k][head + 1]], axis=1)
            total += dot(context, panel, MINOR_BOTH)
    refs[4][...] = total


def delta_kernel(slots_ref, near_ref, far_ref, *refs):
    out_ref, stage_ref, sems = refs[4:]
    me = lax.axis_index("req")
    first = (slots_ref[me >> 1] ^ me) & 3
    rank = (near_ref[...] + far_ref[...]).astype(jnp.bfloat16)
    wide = stage_ref.shape[2]
    copies = []
    for k in range(4):
        panel = jnp.concatenate([refs[k][b] for b in range(refs[k].shape[0])], axis=1)
        stage_ref[k] = (2.0 * dot(rank, panel)).astype(jnp.bfloat16)
        columns = pl.ds(pl.multiple_of((first ^ k) * wide, HEAD_SIZE), wide)
        copy = pltpu.make_async_copy(stage_ref.at[k], out_ref.at[:, columns], sems.at[k])
        copy.start()
        copies.append(copy)
    for copy in copies:
        copy.wait()


def delta_of(slots, near, far, panels):
    rows = near.shape[0]
    wide = panels[0].shape[0] * panels[0].shape[2]
    return pl.pallas_call(
        delta_kernel,
        in_specs=[pl.BlockSpec(memory_space=pltpu.SMEM)]
        + [pl.BlockSpec(memory_space=pltpu.VMEM)] * 6,
        out_specs=pl.BlockSpec(memory_space=pl.ANY),
        out_shape=jax.ShapeDtypeStruct((rows, 4 * wide), jnp.bfloat16),
        scratch_shapes=[pltpu.VMEM((4, rows, wide), jnp.bfloat16), pltpu.SemaphoreType.DMA((4,))],
        compiler_params=pltpu.CompilerParams(vmem_limit_bytes=VMEM_LIMIT),
        name="delta",
    )(slots, near, far, *panels)


def quarter_cut(blocks):
    count = blocks.shape[0] // 4
    return [blocks[k * count : (k + 1) * count] for k in range(4)]


def spread(cut):
    return cut[:1] + [swapped(cut[k], "req", k) for k in (1, 2, 3)]


def cross(slots, quarters, weight=0):
    shape = jax.ShapeDtypeStruct((2, *quarters[0].shape), quarters[0].dtype)
    return in_vmem(cross_kernel, "cross", shape, slots, *quarters, weight=weight)


def gather(slots, quarters, came):
    shape = jax.ShapeDtypeStruct(quarters[0].shape, quarters[0].dtype)
    near, aside = in_vmem(settle_kernel, "settle", [shape] * 2, slots, *quarters, came)
    return [near] + [swapped(panel, "req", k) for k, panel in ((1, near), (2, aside), (3, aside))]


def after(earlier, value):
    return lax.optimization_barrier((earlier, value))[1]


def eight_way(queries, keys, values, down, up, request_adapter, adapter_slot_table):
    slots = slots_of(request_adapter, adapter_slot_table)
    down_quarters = spread(quarter_cut(down))
    up_cut = quarter_cut(after(slots, up))
    far = swapped(jnp.concatenate(after(up_cut, (keys, values)), axis=1), "req", 1)
    down_sent = cross(slots, down_quarters, 3000000000)
    down_came = swapped(down_sent, "req", 4)
    up_quarters = spread(after(down_sent, up_cut))
    context = attend(queries, keys, values, far)
    down_panels = gather(slots, down_quarters, down_came)
    up_came = swapped(cross(slots, after(context, up_quarters)), "req", 4)
    up_panels = gather(slots, up_quarters, up_came)
    rank_shape = jax.ShapeDtypeStruct((context.shape[1], ADAPTER_RANK), jnp.float32)
    rank = in_vmem(rank_kernel, "rank_mix", rank_shape, slots, context, *down_panels)
    return delta_of(slots, rank, swapped(rank, "tp", 1), up_panels)


def any_way(context, down, up, slots):
    partner_count = lax.axis_size("req")
    rows = context.shape[1]

    def exchanged(blocks):
        slot_count, block_count = blocks.shape[:2]
        tail = blocks.shape[2] // partner_count
        cut = blocks.reshape(slot_count, block_count, partner_count, tail, blocks.shape[3])
        cut = jnp.moveaxis(cut, 2, 1)
        library = lax.all_to_all(cut, "req", split_axis=1, concat_axis=0, tiled=True)[:, 0]
        wanted = jnp.take(library, slots[jnp.arange(partner_count) // 2], axis=0)
        return lax.all_to_all(wanted, "req", split_axis=0, concat_axis=0, tiled=True)

    down_all = exchanged(jnp.swapaxes(down, 2, 3))
    up_all = exchanged(jnp.swapaxes(up, 2, 3))
    flat = jnp.swapaxes(context, 0, 1).reshape(rows, down_all.shape[1], partner_count, down_all.shape[2])
    rank = jnp.einsum("thrp,rhpk->tk", flat, down_all, preferred_element_type=jnp.float32)
    rank = lax.psum(rank, "tp").astype(jnp.bfloat16)
    mixed = jnp.einsum("tk,rblk->tbrl", rank, up_all, preferred_element_type=jnp.float32)
    return (2.0 * mixed.reshape(rows, -1)).astype(jnp.bfloat16)


def body(
    projected_queries,
    projected_keys,
    projected_values,
    request_adapter,
    adapter_slot_table,
    adapter_down_factor,
    adapter_up_factor,
):
    down = jnp.swapaxes(adapter_down_factor, 2, 3)
    up = jnp.swapaxes(adapter_up_factor, 1, 2)
    spans = (projected_queries, projected_keys, projected_values)
    if lax.axis_size("req") == 8 and down.shape[0] == 1:
        return eight_way(*spans, down[0], up[0], request_adapter, adapter_slot_table)
    far = swapped(jnp.concatenate(spans[1:], axis=1), "req", 1)
    return any_way(attend(*spans, far), down, up, adapter_slot_table[request_adapter])


def solution(mesh):
    placed = (
        P(("groups", "req"), "tp"),
        P(("groups", "req"), "tp"),
        P(("groups", "req"), "tp"),
        P("groups"),
        P("groups"),
        P(("groups", "req"), "tp", None, None),
        P(("groups", "req"), None, "tp", None),
    )
    return jax.shard_map(
        body, mesh=mesh, in_specs=placed, out_specs=P(("groups", "req"), "tp"), check_vma=False
    )
```

```python
import functools
import math

import jax
import jax.numpy as jnp
from jax import lax
from jax.experimental import pallas as pl
from jax.experimental.pallas import tpu as pltpu
from jax.sharding import PartitionSpec as P

QUERY_HEAD_COUNT = 64
KEY_VALUE_HEADS = 8
HEAD_SIZE = 128
ADAPTER_RANK = 64
GROUP = QUERY_HEAD_COUNT // KEY_VALUE_HEADS
EXP2_SCALE = math.log2(math.e) / math.sqrt(HEAD_SIZE)
VMEM_LIMIT = 32 << 20
WEIGHT = 3_000_000_000
MINOR_BOTH = (((1,), (1,)), ((), ()))
PLAIN = (((1,), (0,)), ((), ()))


def dot(lhs, rhs, dims=PLAIN):
    return lax.dot_general(lhs, rhs, dims, preferred_element_type=jnp.float32)


def swapped(shard, axis, mask):
    size = lax.axis_size(axis)
    return lax.ppermute(shard, axis, [(i, i ^ mask) for i in range(size)])


def attend_kernel(query_ref, key_ref, value_ref, far_ref, context_ref):
    rows = key_ref.shape[0]
    ones = jnp.ones((rows, HEAD_SIZE), jnp.bfloat16)
    causal = lax.broadcasted_iota(jnp.int32, (rows, rows), 0) >= lax.broadcasted_iota(
        jnp.int32, (rows, rows), 1
    )

    def run(with_far):
        for group in range(context_ref.shape[0]):
            own = slice(group * HEAD_SIZE, (group + 1) * HEAD_SIZE)
            near_key = key_ref[:, own]
            near_value = jnp.concatenate([value_ref[:, own], ones], axis=1)
            if with_far:
                far_key = far_ref[:, own]
                far_value = jnp.concatenate([far_ref[:, key_ref.shape[1] + group * HEAD_SIZE : key_ref.shape[1] + (group + 1) * HEAD_SIZE], ones], axis=1)
            for head in range(GROUP):
                at = (group * GROUP + head) * HEAD_SIZE
                query = query_ref[:, at : at + HEAD_SIZE]
                near = jnp.where(causal, dot(query, near_key, MINOR_BOTH), -1e30)
                peak = jnp.max(near, axis=1, keepdims=True)
                if with_far:
                    far = dot(query, far_key, MINOR_BOTH)
                    peak = jnp.maximum(peak, jnp.max(far, axis=1, keepdims=True))
                out = dot(jnp.exp2((near - peak) * EXP2_SCALE).astype(jnp.bfloat16), near_value)
                if with_far:
                    out += dot(jnp.exp2((far - peak) * EXP2_SCALE).astype(jnp.bfloat16), far_value)
                context = (out[:, :HEAD_SIZE] / out[:, HEAD_SIZE:]).astype(jnp.bfloat16)
                context_ref[group, :, head * HEAD_SIZE : (head + 1) * HEAD_SIZE] = context

    parity = lax.axis_index("req") & 1

    @pl.when(parity == 0)
    def _():
        run(False)

    @pl.when(parity != 0)
    def _():
        run(True)


def attend(queries, keys, values, far):
    rows, width = queries.shape
    shape = (keys.shape[1] // HEAD_SIZE, rows, GROUP * HEAD_SIZE)
    whole = jax.ShapeDtypeStruct(shape, jnp.bfloat16)
    return in_vmem(attend_kernel, "attend", whole, None, queries, keys, values, far)


def in_vmem(kernel, name, out_shape, slots, *arrays, weight=0):
    scalars = [] if slots is None else [slots]
    return pl.pallas_call(
        kernel,
        in_specs=[pl.BlockSpec(memory_space=pltpu.SMEM)] * len(scalars)
        + [pl.BlockSpec(memory_space=pltpu.VMEM)] * len(arrays),
        out_specs=jax.tree.map(lambda _: pl.BlockSpec(memory_space=pltpu.VMEM), out_shape),
        out_shape=out_shape,
        compiler_params=pltpu.CompilerParams(vmem_limit_bytes=VMEM_LIMIT),
        cost_estimate=pl.CostEstimate(flops=weight, bytes_accessed=weight // 100, transcendentals=0),
        name=name,
    )(*scalars, *arrays)


def slots_kernel(adapter_ref, table_ref, slots_ref):
    for request in range(slots_ref.shape[0]):
        slots_ref[request] = table_ref[adapter_ref[request]]


def slots_of(request_adapter, adapter_slot_table):
    return pl.pallas_call(
        slots_kernel,
        in_specs=[pl.BlockSpec(memory_space=pltpu.SMEM)] * 2,
        out_specs=pl.BlockSpec(memory_space=pltpu.SMEM),
        out_shape=jax.ShapeDtypeStruct(request_adapter.shape, jnp.int32),
        cost_estimate=pl.CostEstimate(flops=0, bytes_accessed=0, transcendentals=0),
        name="slots",
    )(request_adapter, adapter_slot_table)


def take(request, me, slots_ref, quarter_refs, out_ref, at, other=None):
    where = slots_ref[request] ^ me
    for k in range(4):

        @pl.when((where if other is not None else where & 3) == k)
        def _():
            out_ref[at] = quarter_refs[k][...]

    if other is not None:

        @pl.when(where >= 4)
        def _():
            out_ref[at] = other[...]


def choose_kernel(slots_ref, *refs):
    me = lax.axis_index("req")
    for apart in (1, 2, 3):
        take((me >> 1) ^ apart, me, slots_ref, refs[:4], refs[3 + apart], ...)


def assemble_kernel(slots_ref, *refs):
    me = lax.axis_index("req")
    where = slots_ref[me >> 1] ^ me
    for k in range(4):

        @pl.when(where == k)
        def _():
            refs[7][0] = refs[k][...]
            refs[7][1] = refs[4][...]

    @pl.when(where >= 4)
    def _():
        refs[7][0] = refs[5][...]
        refs[7][1] = refs[6][...]


def cross_kernel(slots_ref, *refs):
    me = lax.axis_index("req")
    for at in range(2):
        take((me >> 1) ^ (2 + at), me, slots_ref, refs[:4], refs[4], at)


def settle_kernel(slots_ref, *refs):
    me = lax.axis_index("req")
    for at in range(2):
        request = (me >> 1) ^ at
        take(request, me, slots_ref, refs[:4], refs[5 + at], ..., refs[4].at[at])


def rank_kernel(slots_ref, context_ref, held_ref, got_ref, rank_ref):
    me = lax.axis_index("req")
    first = (slots_ref[me >> 1] ^ me) & 3
    total = jnp.zeros(rank_ref.shape, jnp.float32)
    for k in range(4):
        panel_ref = (held_ref, got_ref)[k & 1].at[k >> 1]
        for head in range(0, GROUP, 2):
            context = context_ref[first ^ k, :, head * HEAD_SIZE : (head + 2) * HEAD_SIZE]
            panel = jnp.concatenate([panel_ref[head], panel_ref[head + 1]], axis=1)
            total += dot(context, panel, MINOR_BOTH)
    rank_ref[...] = total


def delta_kernel(slots_ref, near_ref, far_ref, *refs):
    out_ref, stage_ref, sems = refs[4:]
    me = lax.axis_index("req")
    first = (slots_ref[me >> 1] ^ me) & 3
    first = (first >> 1) | ((first & 1) << 1)
    rank = (near_ref[...] + far_ref[...]).astype(jnp.bfloat16)
    wide = stage_ref.shape[2]
    copies = []
    for k in range(4):
        panel = jnp.concatenate([refs[k][b] for b in range(refs[k].shape[0])], axis=1)
        stage_ref[k] = (2.0 * dot(rank, panel)).astype(jnp.bfloat16)
        columns = pl.ds(pl.multiple_of((first ^ (k >> 1) ^ ((k & 1) << 1)) * wide, HEAD_SIZE), wide)
        copy = pltpu.make_async_copy(stage_ref.at[k], out_ref.at[:, columns], sems.at[k])
        copy.start()
        copies.append(copy)
    for copy in copies:
        copy.wait()


def delta_of(slots, near, far, panels):
    rows = near.shape[0]
    wide = panels[0].shape[0] * panels[0].shape[2]
    return pl.pallas_call(
        delta_kernel,
        in_specs=[pl.BlockSpec(memory_space=pltpu.SMEM)]
        + [pl.BlockSpec(memory_space=pltpu.VMEM)] * 6,
        out_specs=pl.BlockSpec(memory_space=pl.ANY),
        out_shape=jax.ShapeDtypeStruct((rows, 4 * wide), jnp.bfloat16),
        scratch_shapes=[pltpu.VMEM((4, rows, wide), jnp.bfloat16), pltpu.SemaphoreType.DMA((4,))],
        compiler_params=pltpu.CompilerParams(vmem_limit_bytes=VMEM_LIMIT),
        name="delta",
    )(slots, near, far, *panels)


def quarter_cut(blocks):
    count = blocks.shape[0] // 4
    return [blocks[k * count : (k + 1) * count] for k in range(4)]


def spread(cut):
    return cut[:1] + [swapped(cut[k], "req", k) for k in (1, 2, 3)]


def cross(slots, quarters, weight=0):
    shape = jax.ShapeDtypeStruct((2, *quarters[0].shape), quarters[0].dtype)
    return in_vmem(cross_kernel, "cross", shape, slots, *quarters, weight=weight)


def gather(slots, quarters, came, weight=0):
    shape = jax.ShapeDtypeStruct(quarters[0].shape, quarters[0].dtype)
    near, aside = in_vmem(settle_kernel, "settle", [shape] * 2, slots, *quarters, came, weight=weight)
    return [near] + [swapped(panel, "req", k) for k, panel in ((1, near), (2, aside), (3, aside))]


def after(earlier, value):
    return lax.optimization_barrier((earlier, value))[1]


def spread_in_turn(over_x, own, earlier):
    count = own.shape[0] // 2
    over_x = after(earlier, over_x)
    over_z = swapped(jnp.concatenate([own[count:], over_x[count:]]), "req", 2)
    return [own[:count], over_x[:count], over_z[:count], over_z[count:]]


def deliver(slots, quarters):
    shape = jax.ShapeDtypeStruct(quarters[0].shape, quarters[0].dtype)
    sent = in_vmem(choose_kernel, "choose", [shape] * 3, slots, *quarters, weight=WEIGHT)
    return sent, [swapped(panel, "req", 2 * apart) for apart, panel in enumerate(sent, 1)]


def assemble(slots, quarters, came):
    both = jax.ShapeDtypeStruct((2, *came[0].shape), came[0].dtype)
    return in_vmem(assemble_kernel, "assemble", both, slots, *quarters, *came)


def eight_way(queries, keys, values, down, up, request_adapter, adapter_slot_table):
    slots = slots_of(request_adapter, adapter_slot_table)
    down_cut = quarter_cut(down)
    down_quarters = spread(down_cut)
    half = up.shape[0] // 2
    up = after(down_cut, up)
    up_half, up_own = up[half:], up[:half]
    up_over_x = swapped(up_half, "req", 1)
    far = jnp.concatenate(after(up_half, (keys, values)), axis=1)
    far = swapped(far, "req", 1)
    down_sent, down_came = deliver(slots, down_quarters)
    up_quarters = spread_in_turn(up_over_x, up_own, down_sent)
    down_held = assemble(slots, down_quarters, down_came)
    down_got = swapped(down_held, "req", 1)
    up_sent = cross(slots, after(down_held, up_quarters))
    up_came = swapped(up_sent, "req", 4)
    context = attend(queries, keys, values, after(up_sent, far))
    up_panels = gather(slots, up_quarters, after(context, up_came), 1000_000_000)
    rank_shape = jax.ShapeDtypeStruct((context.shape[1], ADAPTER_RANK), jnp.float32)
    rank = in_vmem(rank_kernel, "rank_mix", rank_shape, slots, context, down_held, down_got)
    return delta_of(slots, rank, swapped(rank, "tp", 1), up_panels)


def any_way(context, down, up, slots):
    partner_count = lax.axis_size("req")
    rows = context.shape[1]

    def exchanged(blocks):
        slot_count, block_count = blocks.shape[:2]
        tail = blocks.shape[2] // partner_count
        cut = blocks.reshape(slot_count, block_count, partner_count, tail, blocks.shape[3])
        cut = jnp.moveaxis(cut, 2, 1)
        library = lax.all_to_all(cut, "req", split_axis=1, concat_axis=0, tiled=True)[:, 0]
        wanted = jnp.take(library, slots[jnp.arange(partner_count) // 2], axis=0)
        return lax.all_to_all(wanted, "req", split_axis=0, concat_axis=0, tiled=True)

    down_all = exchanged(jnp.swapaxes(down, 2, 3))
    up_all = exchanged(jnp.swapaxes(up, 2, 3))
    flat = jnp.swapaxes(context, 0, 1).reshape(rows, down_all.shape[1], partner_count, down_all.shape[2])
    rank = jnp.einsum("thrp,rhpk->tk", flat, down_all, preferred_element_type=jnp.float32)
    rank = lax.psum(rank, "tp").astype(jnp.bfloat16)
    mixed = jnp.einsum("tk,rblk->tbrl", rank, up_all, preferred_element_type=jnp.float32)
    return (2.0 * mixed.reshape(rows, -1)).astype(jnp.bfloat16)


def body(
    projected_queries,
    projected_keys,
    projected_values,
    request_adapter,
    adapter_slot_table,
    adapter_down_factor,
    adapter_up_factor,
):
    down = jnp.swapaxes(adapter_down_factor, 2, 3)
    up = jnp.swapaxes(adapter_up_factor, 1, 2)
    spans = (projected_queries, projected_keys, projected_values)
    if lax.axis_size("req") == 8 and down.shape[0] == 1:
        return eight_way(*spans, down[0], up[0], request_adapter, adapter_slot_table)
    far = swapped(jnp.concatenate(spans[1:], axis=1), "req", 1)
    return any_way(attend(*spans, far), down, up, adapter_slot_table[request_adapter])


def solution(mesh):
    placed = (
        P(("groups", "req"), "tp"),
        P(("groups", "req"), "tp"),
        P(("groups", "req"), "tp"),
        P("groups"),
        P("groups"),
        P(("groups", "req"), "tp", None, None),
        P(("groups", "req"), None, "tp", None),
    )
    return jax.shard_map(
        body, mesh=mesh, in_specs=placed, out_specs=P(("groups", "req"), "tp"), check_vma=False
    )
```

```python
import functools
import math

import jax
import jax.numpy as jnp
from jax import lax
from jax.experimental import pallas as pl
from jax.experimental.pallas import tpu as pltpu
from jax.sharding import PartitionSpec as P

QUERY_HEAD_COUNT = 64
KEY_VALUE_HEADS = 8
HEAD_SIZE = 128
ADAPTER_RANK = 64
GROUP = QUERY_HEAD_COUNT // KEY_VALUE_HEADS
EXP2_SCALE = math.log2(math.e) / math.sqrt(HEAD_SIZE)
VMEM_LIMIT = 32 << 20
WEIGHT = 3_000_000_000
MINOR_BOTH = (((1,), (1,)), ((), ()))
PLAIN = (((1,), (0,)), ((), ()))


def dot(lhs, rhs, dims=PLAIN):
    return lax.dot_general(lhs, rhs, dims, preferred_element_type=jnp.float32)


def swapped(shard, axis, mask):
    size = lax.axis_size(axis)
    return lax.ppermute(shard, axis, [(i, i ^ mask) for i in range(size)])


def attend_kernel(query_ref, key_ref, value_ref, far_ref, context_ref):
    rows = key_ref.shape[0]
    ones = jnp.ones((rows, HEAD_SIZE), jnp.bfloat16)
    causal = lax.broadcasted_iota(jnp.int32, (rows, rows), 0) >= lax.broadcasted_iota(
        jnp.int32, (rows, rows), 1
    )

    def run(with_far):
        for group in range(context_ref.shape[0]):
            own = slice(group * HEAD_SIZE, (group + 1) * HEAD_SIZE)
            near_key = key_ref[:, own]
            near_value = jnp.concatenate([value_ref[:, own], ones], axis=1)
            if with_far:
                far_key = far_ref[:, own]
                far_value = jnp.concatenate([far_ref[:, key_ref.shape[1] + group * HEAD_SIZE : key_ref.shape[1] + (group + 1) * HEAD_SIZE], ones], axis=1)
            for head in range(GROUP):
                at = (group * GROUP + head) * HEAD_SIZE
                query = query_ref[:, at : at + HEAD_SIZE]
                near = jnp.where(causal, dot(query, near_key, MINOR_BOTH), -1e30)
                peak = jnp.max(near, axis=1, keepdims=True)
                if with_far:
                    far = dot(query, far_key, MINOR_BOTH)
                    peak = jnp.maximum(peak, jnp.max(far, axis=1, keepdims=True))
                out = dot(jnp.exp2((near - peak) * EXP2_SCALE).astype(jnp.bfloat16), near_value)
                if with_far:
                    out += dot(jnp.exp2((far - peak) * EXP2_SCALE).astype(jnp.bfloat16), far_value)
                context = (out[:, :HEAD_SIZE] / out[:, HEAD_SIZE:]).astype(jnp.bfloat16)
                context_ref[group, :, head * HEAD_SIZE : (head + 1) * HEAD_SIZE] = context

    parity = lax.axis_index("req") & 1

    @pl.when(parity == 0)
    def _():
        run(False)

    @pl.when(parity != 0)
    def _():
        run(True)


def attend(queries, keys, values, far):
    rows, width = queries.shape
    shape = (keys.shape[1] // HEAD_SIZE, rows, GROUP * HEAD_SIZE)
    whole = jax.ShapeDtypeStruct(shape, jnp.bfloat16)
    return in_vmem(attend_kernel, "attend", whole, None, queries, keys, values, far)


def in_vmem(kernel, name, out_shape, slots, *arrays, weight=0):
    scalars = [] if slots is None else [slots]
    return pl.pallas_call(
        kernel,
        in_specs=[pl.BlockSpec(memory_space=pltpu.SMEM)] * len(scalars)
        + [pl.BlockSpec(memory_space=pltpu.VMEM)] * len(arrays),
        out_specs=jax.tree.map(lambda _: pl.BlockSpec(memory_space=pltpu.VMEM), out_shape),
        out_shape=out_shape,
        compiler_params=pltpu.CompilerParams(vmem_limit_bytes=VMEM_LIMIT),
        cost_estimate=pl.CostEstimate(flops=weight, bytes_accessed=weight // 100, transcendentals=0),
        name=name,
    )(*scalars, *arrays)


def slots_kernel(adapter_ref, table_ref, slots_ref):
    for request in range(slots_ref.shape[0]):
        slots_ref[request] = table_ref[adapter_ref[request]]


def slots_of(request_adapter, adapter_slot_table):
    return pl.pallas_call(
        slots_kernel,
        in_specs=[pl.BlockSpec(memory_space=pltpu.SMEM)] * 2,
        out_specs=pl.BlockSpec(memory_space=pltpu.SMEM),
        out_shape=jax.ShapeDtypeStruct(request_adapter.shape, jnp.int32),
        cost_estimate=pl.CostEstimate(flops=0, bytes_accessed=0, transcendentals=0),
        name="slots",
    )(request_adapter, adapter_slot_table)


def take(request, me, slots_ref, quarter_refs, out_ref, at, other=None):
    where = slots_ref[request] ^ me
    for k in range(4):

        @pl.when((where if other is not None else where & 3) == k)
        def _():
            out_ref[at] = quarter_refs[k][...]

    if other is not None:

        @pl.when(where >= 4)
        def _():
            out_ref[at] = other[...]


def choose_kernel(slots_ref, *refs):
    me = lax.axis_index("req")
    for apart in (1, 2, 3):
        take((me >> 1) ^ apart, me, slots_ref, refs[:4], refs[3 + apart], ...)


def assemble_kernel(slots_ref, *refs):
    me = lax.axis_index("req")
    where = slots_ref[me >> 1] ^ me
    for k in range(4):

        @pl.when(where == k)
        def _():
            refs[7][0] = refs[k][...]
            refs[7][1] = refs[4][...]

    @pl.when(where >= 4)
    def _():
        refs[7][0] = refs[5][...]
        refs[7][1] = refs[6][...]


def rank_kernel(slots_ref, context_ref, held_ref, got_ref, rank_ref):
    me = lax.axis_index("req")
    first = (slots_ref[me >> 1] ^ me) & 3
    total = jnp.zeros(rank_ref.shape, jnp.float32)
    for k in range(4):
        panel_ref = (held_ref, got_ref)[k & 1].at[k >> 1]
        for head in range(0, GROUP, 2):
            context = context_ref[first ^ k, :, head * HEAD_SIZE : (head + 2) * HEAD_SIZE]
            panel = jnp.concatenate([panel_ref[head], panel_ref[head + 1]], axis=1)
            total += dot(context, panel, MINOR_BOTH)
    rank_ref[...] = total


def delta_kernel(slots_ref, near_ref, far_ref, *refs):
    out_ref, stage_ref, sems = refs[2:]
    me = lax.axis_index("req")
    first = (slots_ref[me >> 1] ^ me) & 3
    first = (first >> 1) | ((first & 1) << 1)
    rank = (near_ref[...] + far_ref[...]).astype(jnp.bfloat16)
    wide = stage_ref.shape[2]
    copies = []
    for k in (0, 2, 1, 3):
        panel_ref = refs[k & 1].at[k >> 1]
        panel = jnp.concatenate([panel_ref[b] for b in range(panel_ref.shape[0])], axis=1)
        stage_ref[k] = (2.0 * dot(rank, panel)).astype(jnp.bfloat16)
        columns = pl.ds(pl.multiple_of((first ^ (k >> 1) ^ ((k & 1) << 1)) * wide, HEAD_SIZE), wide)
        copy = pltpu.make_async_copy(stage_ref.at[k], out_ref.at[:, columns], sems.at[k])
        copy.start()
        copies.append(copy)
    for copy in copies:
        copy.wait()


def delta_of(slots, near, far, held, got):
    rows = near.shape[0]
    wide = held.shape[1] * held.shape[3]
    return pl.pallas_call(
        delta_kernel,
        in_specs=[pl.BlockSpec(memory_space=pltpu.SMEM)]
        + [pl.BlockSpec(memory_space=pltpu.VMEM)] * 4,
        out_specs=pl.BlockSpec(memory_space=pl.ANY),
        out_shape=jax.ShapeDtypeStruct((rows, 4 * wide), jnp.bfloat16),
        scratch_shapes=[pltpu.VMEM((4, rows, wide), jnp.bfloat16), pltpu.SemaphoreType.DMA((4,))],
        compiler_params=pltpu.CompilerParams(vmem_limit_bytes=VMEM_LIMIT),
        name="delta",
    )(slots, near, far, held, got)


def quarter_cut(blocks):
    count = blocks.shape[0] // 4
    return [blocks[k * count : (k + 1) * count] for k in range(4)]


def spread(cut):
    return cut[:1] + [swapped(cut[k], "req", k) for k in (1, 2, 3)]


def after(earlier, value):
    return lax.optimization_barrier((earlier, value))[1]


def spread_in_turn(over_x, own, earlier):
    count = own.shape[0] // 2
    over_x = after(earlier, over_x)
    over_z = swapped(jnp.concatenate([own[count:], over_x[count:]]), "req", 2)
    return [own[:count], over_x[:count], over_z[:count], over_z[count:]]


def deliver(slots, quarters, weight=0):
    shape = jax.ShapeDtypeStruct(quarters[0].shape, quarters[0].dtype)
    sent = in_vmem(choose_kernel, "choose", [shape] * 3, slots, *quarters, weight=weight)
    return sent, [swapped(panel, "req", 2 * apart) for apart, panel in enumerate(sent, 1)]


def assemble(slots, quarters, came, weight=0):
    both = jax.ShapeDtypeStruct((2, *came[0].shape), came[0].dtype)
    return in_vmem(assemble_kernel, "assemble", both, slots, *quarters, *came, weight=weight)


def eight_way(queries, keys, values, down, up, request_adapter, adapter_slot_table):
    slots = slots_of(request_adapter, adapter_slot_table)
    down_cut = quarter_cut(down)
    down_quarters = spread(down_cut)
    half = up.shape[0] // 2
    up = after(down_cut, up)
    up_half, up_own = up[half:], up[:half]
    up_over_x = swapped(up_half, "req", 1)
    down_sent, down_came = deliver(slots, down_quarters, WEIGHT)
    far = swapped(jnp.concatenate(after(down_sent, (keys, values)), axis=1), "req", 1)
    up_quarters = spread_in_turn(up_over_x, up_own, down_sent)
    down_held = assemble(slots, down_quarters, down_came, 3000_000_000)
    down_got = swapped(down_held, "req", 1)
    up_sent, up_came = deliver(slots, after(down_held, up_quarters))
    context = attend(queries, keys, values, after(up_sent, far))
    up_held = assemble(slots, up_quarters, after(context, up_came), 1000_000_000)
    up_got = swapped(up_held, "req", 1)
    rank_shape = jax.ShapeDtypeStruct((context.shape[1], ADAPTER_RANK), jnp.float32)
    rank = in_vmem(rank_kernel, "rank_mix", rank_shape, slots, context, down_held, down_got)
    return delta_of(slots, rank, swapped(rank, "tp", 1), up_held, up_got)


def any_way(context, down, up, slots):
    partner_count = lax.axis_size("req")
    rows = context.shape[1]

    def exchanged(blocks):
        slot_count, block_count = blocks.shape[:2]
        tail = blocks.shape[2] // partner_count
        cut = blocks.reshape(slot_count, block_count, partner_count, tail, blocks.shape[3])
        cut = jnp.moveaxis(cut, 2, 1)
        library = lax.all_to_all(cut, "req", split_axis=1, concat_axis=0, tiled=True)[:, 0]
        wanted = jnp.take(library, slots[jnp.arange(partner_count) // 2], axis=0)
        return lax.all_to_all(wanted, "req", split_axis=0, concat_axis=0, tiled=True)

    down_all = exchanged(jnp.swapaxes(down, 2, 3))
    up_all = exchanged(jnp.swapaxes(up, 2, 3))
    flat = jnp.swapaxes(context, 0, 1).reshape(rows, down_all.shape[1], partner_count, down_all.shape[2])
    rank = jnp.einsum("thrp,rhpk->tk", flat, down_all, preferred_element_type=jnp.float32)
    rank = lax.psum(rank, "tp").astype(jnp.bfloat16)
    mixed = jnp.einsum("tk,rblk->tbrl", rank, up_all, preferred_element_type=jnp.float32)
    return (2.0 * mixed.reshape(rows, -1)).astype(jnp.bfloat16)


def body(
    projected_queries,
    projected_keys,
    projected_values,
    request_adapter,
    adapter_slot_table,
    adapter_down_factor,
    adapter_up_factor,
):
    down = jnp.swapaxes(adapter_down_factor, 2, 3)
    up = jnp.swapaxes(adapter_up_factor, 1, 2)
    spans = (projected_queries, projected_keys, projected_values)
    if lax.axis_size("req") == 8 and down.shape[0] == 1:
        return eight_way(*spans, down[0], up[0], request_adapter, adapter_slot_table)
    far = swapped(jnp.concatenate(spans[1:], axis=1), "req", 1)
    return any_way(attend(*spans, far), down, up, adapter_slot_table[request_adapter])


def solution(mesh):
    placed = (
        P(("groups", "req"), "tp"),
        P(("groups", "req"), "tp"),
        P(("groups", "req"), "tp"),
        P("groups"),
        P("groups"),
        P(("groups", "req"), "tp", None, None),
        P(("groups", "req"), None, "tp", None),
    )
    return jax.shard_map(
        body, mesh=mesh, in_specs=placed, out_specs=P(("groups", "req"), "tp"), check_vma=False
    )
```

```python
import functools
import math

import jax
import jax.numpy as jnp
from jax import lax
from jax.experimental import pallas as pl
from jax.experimental.pallas import tpu as pltpu
from jax.sharding import PartitionSpec as P

QUERY_HEAD_COUNT = 64
KEY_VALUE_HEADS = 8
HEAD_SIZE = 128
ADAPTER_RANK = 64
GROUP = QUERY_HEAD_COUNT // KEY_VALUE_HEADS
EXP2_SCALE = math.log2(math.e) / math.sqrt(HEAD_SIZE)
VMEM_LIMIT = 32 << 20
WEIGHT = 3_000_000_000
MINOR_BOTH = (((1,), (1,)), ((), ()))
PLAIN = (((1,), (0,)), ((), ()))


def dot(lhs, rhs, dims=PLAIN):
    return lax.dot_general(lhs, rhs, dims, preferred_element_type=jnp.float32)


def swapped(shard, axis, mask):
    size = lax.axis_size(axis)
    return lax.ppermute(shard, axis, [(i, i ^ mask) for i in range(size)])


def attend_kernel(query_ref, key_ref, value_ref, far_ref, context_ref):
    rows = key_ref.shape[0]
    ones = jnp.ones((rows, HEAD_SIZE), jnp.bfloat16)
    causal = lax.broadcasted_iota(jnp.int32, (rows, rows), 0) >= lax.broadcasted_iota(
        jnp.int32, (rows, rows), 1
    )

    def run(with_far):
        for group in range(context_ref.shape[0]):
            own = slice(group * HEAD_SIZE, (group + 1) * HEAD_SIZE)
            near_key = key_ref[:, own]
            near_value = jnp.concatenate([value_ref[:, own], ones], axis=1)
            if with_far:
                far_key = far_ref[:, own]
                far_value = jnp.concatenate([far_ref[:, key_ref.shape[1] + group * HEAD_SIZE : key_ref.shape[1] + (group + 1) * HEAD_SIZE], ones], axis=1)
            for head in range(GROUP):
                at = (group * GROUP + head) * HEAD_SIZE
                query = query_ref[:, at : at + HEAD_SIZE]
                near = jnp.where(causal, dot(query, near_key, MINOR_BOTH), -1e30)
                peak = jnp.max(near, axis=1, keepdims=True)
                if with_far:
                    far = dot(query, far_key, MINOR_BOTH)
                    peak = jnp.maximum(peak, jnp.max(far, axis=1, keepdims=True))
                out = dot(jnp.exp2((near - peak) * EXP2_SCALE).astype(jnp.bfloat16), near_value)
                if with_far:
                    out += dot(jnp.exp2((far - peak) * EXP2_SCALE).astype(jnp.bfloat16), far_value)
                context = (out[:, :HEAD_SIZE] / out[:, HEAD_SIZE:]).astype(jnp.bfloat16)
                context_ref[group, :, head * HEAD_SIZE : (head + 1) * HEAD_SIZE] = context

    parity = lax.axis_index("req") & 1

    @pl.when(parity == 0)
    def _():
        run(False)

    @pl.when(parity != 0)
    def _():
        run(True)


def attend(queries, keys, values, far):
    rows, width = queries.shape
    shape = (keys.shape[1] // HEAD_SIZE, rows, GROUP * HEAD_SIZE)
    whole = jax.ShapeDtypeStruct(shape, jnp.bfloat16)
    return in_vmem(attend_kernel, "attend", whole, None, queries, keys, values, far)


def in_vmem(kernel, name, out_shape, slots, *arrays, weight=0):
    scalars = [] if slots is None else [slots]
    return pl.pallas_call(
        kernel,
        in_specs=[pl.BlockSpec(memory_space=pltpu.SMEM)] * len(scalars)
        + [pl.BlockSpec(memory_space=pltpu.VMEM)] * len(arrays),
        out_specs=jax.tree.map(lambda _: pl.BlockSpec(memory_space=pltpu.VMEM), out_shape),
        out_shape=out_shape,
        compiler_params=pltpu.CompilerParams(vmem_limit_bytes=VMEM_LIMIT),
        cost_estimate=pl.CostEstimate(flops=weight, bytes_accessed=weight // 100, transcendentals=0),
        name=name,
    )(*scalars, *arrays)


def slots_kernel(adapter_ref, table_ref, slots_ref):
    for request in range(slots_ref.shape[0]):
        slots_ref[request] = table_ref[adapter_ref[request]]


def slots_of(request_adapter, adapter_slot_table):
    return pl.pallas_call(
        slots_kernel,
        in_specs=[pl.BlockSpec(memory_space=pltpu.SMEM)] * 2,
        out_specs=pl.BlockSpec(memory_space=pltpu.SMEM),
        out_shape=jax.ShapeDtypeStruct(request_adapter.shape, jnp.int32),
        cost_estimate=pl.CostEstimate(flops=0, bytes_accessed=0, transcendentals=0),
        name="slots",
    )(request_adapter, adapter_slot_table)


def own_kernel(slots_ref, blocks_ref, near_ref, rest_ref):
    del slots_ref
    count = near_ref.shape[0]
    near_ref[...] = blocks_ref[:count]
    rest_ref[...] = blocks_ref[count : 2 * count]


def take(request, me, slots_ref, quarter_refs, out_ref, at, other=None):
    where = slots_ref[request] ^ me
    for k in range(4):

        @pl.when((where if other is not None else where & 3) == k)
        def _():
            out_ref[at] = quarter_refs[k][...]

    if other is not None:

        @pl.when(where >= 4)
        def _():
            out_ref[at] = other[...]


def choose_kernel(slots_ref, *refs):
    me = lax.axis_index("req")
    for apart in (1, 2, 3):
        take((me >> 1) ^ apart, me, slots_ref, refs[:4], refs[3 + apart], ...)


def assemble_kernel(slots_ref, *refs):
    me = lax.axis_index("req")
    where = slots_ref[me >> 1] ^ me
    for k in range(4):

        @pl.when(where == k)
        def _():
            refs[7][0] = refs[k][...]
            refs[7][1] = refs[4][...]

    @pl.when(where >= 4)
    def _():
        refs[7][0] = refs[5][...]
        refs[7][1] = refs[6][...]


def rank_kernel(slots_ref, context_ref, held_ref, got_ref, rank_ref):
    me = lax.axis_index("req")
    first = (slots_ref[me >> 1] ^ me) & 3
    total = jnp.zeros(rank_ref.shape, jnp.float32)
    for k in range(4):
        panel_ref = (held_ref, got_ref)[k & 1].at[k >> 1]
        for head in range(0, GROUP, 2):
            context = context_ref[first ^ k, :, head * HEAD_SIZE : (head + 2) * HEAD_SIZE]
            panel = jnp.concatenate([panel_ref[head], panel_ref[head + 1]], axis=1)
            total += dot(context, panel, MINOR_BOTH)
    rank_ref[...] = total


def delta_kernel(slots_ref, near_ref, far_ref, *refs):
    out_ref, stage_ref, sems = refs[2:]
    me = lax.axis_index("req")
    first = (slots_ref[me >> 1] ^ me) & 3
    first = (first >> 1) | ((first & 1) << 1)
    rank = (near_ref[...] + far_ref[...]).astype(jnp.bfloat16)
    wide = stage_ref.shape[2]
    copies = []
    for k in (0, 2, 1, 3):
        panel_ref = refs[k & 1].at[k >> 1]
        panel = jnp.concatenate([panel_ref[b] for b in range(panel_ref.shape[0])], axis=1)
        stage_ref[k] = (2.0 * dot(rank, panel)).astype(jnp.bfloat16)
        columns = pl.ds(pl.multiple_of((first ^ (k >> 1) ^ ((k & 1) << 1)) * wide, HEAD_SIZE), wide)
        copy = pltpu.make_async_copy(stage_ref.at[k], out_ref.at[:, columns], sems.at[k])
        copy.start()
        copies.append(copy)
    for copy in copies:
        copy.wait()


def delta_of(slots, near, far, held, got):
    rows = near.shape[0]
    wide = held.shape[1] * held.shape[3]
    return pl.pallas_call(
        delta_kernel,
        in_specs=[pl.BlockSpec(memory_space=pltpu.SMEM)]
        + [pl.BlockSpec(memory_space=pltpu.VMEM)] * 4,
        out_specs=pl.BlockSpec(memory_space=pl.ANY),
        out_shape=jax.ShapeDtypeStruct((rows, 4 * wide), jnp.bfloat16),
        scratch_shapes=[pltpu.VMEM((4, rows, wide), jnp.bfloat16), pltpu.SemaphoreType.DMA((4,))],
        compiler_params=pltpu.CompilerParams(vmem_limit_bytes=VMEM_LIMIT),
        name="delta",
    )(slots, near, far, held, got)


def quarter_cut(blocks):
    count = blocks.shape[0] // 4
    return [blocks[k * count : (k + 1) * count] for k in range(4)]


def spread(cut):
    return cut[:1] + [swapped(cut[k], "req", k) for k in (1, 2, 3)]


def after(earlier, value):
    return lax.optimization_barrier((earlier, value))[1]


def spread_in_turn(over_x, own, earlier):
    count = own[0].shape[0]
    over_x = after(earlier, over_x)
    over_z = swapped(jnp.concatenate([own[1], over_x[count:]]), "req", 2)
    return [own[0], over_x[:count], over_z[:count], over_z[count:]]


def deliver(slots, quarters, weight=0):
    shape = jax.ShapeDtypeStruct(quarters[0].shape, quarters[0].dtype)
    sent = in_vmem(choose_kernel, "choose", [shape] * 3, slots, *quarters, weight=weight)
    return sent, [swapped(panel, "req", 2 * apart) for apart, panel in enumerate(sent, 1)]


def assemble(slots, quarters, came, weight=0):
    both = jax.ShapeDtypeStruct((2, *came[0].shape), came[0].dtype)
    return in_vmem(assemble_kernel, "assemble", both, slots, *quarters, *came, weight=weight)


def eight_way(queries, keys, values, down, up, request_adapter, adapter_slot_table):
    slots = slots_of(request_adapter, adapter_slot_table)
    down_cut = quarter_cut(down)
    down_quarters = spread(down_cut)
    half = up.shape[0] // 2
    up = after(down_cut, up)
    up_half = up[half:]
    quarter = jax.ShapeDtypeStruct((half // 2, *up.shape[1:]), up.dtype)
    up_own = in_vmem(own_kernel, "own", [quarter] * 2, slots, up)
    up_over_x = swapped(up_half, "req", 1)
    down_sent, down_came = deliver(slots, down_quarters, WEIGHT)
    far = swapped(jnp.concatenate(after(down_sent, (keys, values)), axis=1), "req", 1)
    up_quarters = spread_in_turn(up_over_x, up_own, down_sent)
    down_held = assemble(slots, down_quarters, down_came, 3000_000_000)
    down_got = swapped(down_held, "req", 1)
    up_sent, up_came = deliver(slots, after(down_held, up_quarters))
    context = attend(queries, keys, values, after(up_sent, far))
    up_held = assemble(slots, up_quarters, after(context, up_came), 1000_000_000)
    up_got = swapped(up_held, "req", 1)
    rank_shape = jax.ShapeDtypeStruct((context.shape[1], ADAPTER_RANK), jnp.float32)
    rank = in_vmem(rank_kernel, "rank_mix", rank_shape, slots, context, down_held, down_got)
    return delta_of(slots, rank, swapped(rank, "tp", 1), up_held, up_got)


def any_way(context, down, up, slots):
    partner_count = lax.axis_size("req")
    rows = context.shape[1]

    def exchanged(blocks):
        slot_count, block_count = blocks.shape[:2]
        tail = blocks.shape[2] // partner_count
        cut = blocks.reshape(slot_count, block_count, partner_count, tail, blocks.shape[3])
        cut = jnp.moveaxis(cut, 2, 1)
        library = lax.all_to_all(cut, "req", split_axis=1, concat_axis=0, tiled=True)[:, 0]
        wanted = jnp.take(library, slots[jnp.arange(partner_count) // 2], axis=0)
        return lax.all_to_all(wanted, "req", split_axis=0, concat_axis=0, tiled=True)

    down_all = exchanged(jnp.swapaxes(down, 2, 3))
    up_all = exchanged(jnp.swapaxes(up, 2, 3))
    flat = jnp.swapaxes(context, 0, 1).reshape(rows, down_all.shape[1], partner_count, down_all.shape[2])
    rank = jnp.einsum("thrp,rhpk->tk", flat, down_all, preferred_element_type=jnp.float32)
    rank = lax.psum(rank, "tp").astype(jnp.bfloat16)
    mixed = jnp.einsum("tk,rblk->tbrl", rank, up_all, preferred_element_type=jnp.float32)
    return (2.0 * mixed.reshape(rows, -1)).astype(jnp.bfloat16)


def body(
    projected_queries,
    projected_keys,
    projected_values,
    request_adapter,
    adapter_slot_table,
    adapter_down_factor,
    adapter_up_factor,
):
    down = jnp.swapaxes(adapter_down_factor, 2, 3)
    up = jnp.swapaxes(adapter_up_factor, 1, 2)
    spans = (projected_queries, projected_keys, projected_values)
    if lax.axis_size("req") == 8 and down.shape[0] == 1:
        return eight_way(*spans, down[0], up[0], request_adapter, adapter_slot_table)
    far = swapped(jnp.concatenate(spans[1:], axis=1), "req", 1)
    return any_way(attend(*spans, far), down, up, adapter_slot_table[request_adapter])


def solution(mesh):
    placed = (
        P(("groups", "req"), "tp"),
        P(("groups", "req"), "tp"),
        P(("groups", "req"), "tp"),
        P("groups"),
        P("groups"),
        P(("groups", "req"), "tp", None, None),
        P(("groups", "req"), None, "tp", None),
    )
    return jax.shard_map(
        body, mesh=mesh, in_specs=placed, out_specs=P(("groups", "req"), "tp"), check_vma=False
    )
```

```python
import functools
import math

import jax
import jax.numpy as jnp
from jax import lax
from jax.experimental import pallas as pl
from jax.experimental.pallas import tpu as pltpu
from jax.sharding import PartitionSpec as P

QUERY_HEAD_COUNT = 64
KEY_VALUE_HEADS = 8
HEAD_SIZE = 128
ADAPTER_RANK = 64
GROUP = QUERY_HEAD_COUNT // KEY_VALUE_HEADS
EXP2_SCALE = math.log2(math.e) / math.sqrt(HEAD_SIZE)
VMEM_LIMIT = 32 << 20
WEIGHT = 3_000_000_000
MINOR_BOTH = (((1,), (1,)), ((), ()))
PLAIN = (((1,), (0,)), ((), ()))


def dot(lhs, rhs, dims=PLAIN):
    return lax.dot_general(lhs, rhs, dims, preferred_element_type=jnp.float32)


def swapped(shard, axis, mask):
    size = lax.axis_size(axis)
    return lax.ppermute(shard, axis, [(i, i ^ mask) for i in range(size)])


def attend_kernel(query_ref, key_ref, value_ref, far_ref, context_ref):
    rows = key_ref.shape[0]
    ones = jnp.ones((rows, HEAD_SIZE), jnp.bfloat16)
    causal = lax.broadcasted_iota(jnp.int32, (rows, rows), 0) >= lax.broadcasted_iota(
        jnp.int32, (rows, rows), 1
    )

    def run(with_far):
        for group in range(context_ref.shape[0]):
            own = slice(group * HEAD_SIZE, (group + 1) * HEAD_SIZE)
            near_key = key_ref[:, own]
            near_value = jnp.concatenate([value_ref[:, own], ones], axis=1)
            if with_far:
                far_key = far_ref[:, own]
                far_value = jnp.concatenate([far_ref[:, key_ref.shape[1] + group * HEAD_SIZE : key_ref.shape[1] + (group + 1) * HEAD_SIZE], ones], axis=1)
            for head in range(GROUP):
                at = (group * GROUP + head) * HEAD_SIZE
                query = query_ref[:, at : at + HEAD_SIZE]
                near = jnp.where(causal, dot(query, near_key, MINOR_BOTH), -1e30)
                peak = jnp.max(near, axis=1, keepdims=True)
                if with_far:
                    far = dot(query, far_key, MINOR_BOTH)
                    peak = jnp.maximum(peak, jnp.max(far, axis=1, keepdims=True))
                out = dot(jnp.exp2((near - peak) * EXP2_SCALE).astype(jnp.bfloat16), near_value)
                if with_far:
                    out += dot(jnp.exp2((far - peak) * EXP2_SCALE).astype(jnp.bfloat16), far_value)
                context = (out[:, :HEAD_SIZE] / out[:, HEAD_SIZE:]).astype(jnp.bfloat16)
                context_ref[group, :, head * HEAD_SIZE : (head + 1) * HEAD_SIZE] = context

    parity = lax.axis_index("req") & 1

    @pl.when(parity == 0)
    def _():
        run(False)

    @pl.when(parity != 0)
    def _():
        run(True)


def attend(queries, keys, values, far):
    rows, width = queries.shape
    shape = (keys.shape[1] // HEAD_SIZE, rows, GROUP * HEAD_SIZE)
    whole = jax.ShapeDtypeStruct(shape, jnp.bfloat16)
    return in_vmem(attend_kernel, "attend", whole, None, queries, keys, values, far)


def in_vmem(kernel, name, out_shape, slots, *arrays, weight=0):
    scalars = [] if slots is None else [slots]
    return pl.pallas_call(
        kernel,
        in_specs=[pl.BlockSpec(memory_space=pltpu.SMEM)] * len(scalars)
        + [pl.BlockSpec(memory_space=pltpu.VMEM)] * len(arrays),
        out_specs=jax.tree.map(lambda _: pl.BlockSpec(memory_space=pltpu.VMEM), out_shape),
        out_shape=out_shape,
        compiler_params=pltpu.CompilerParams(vmem_limit_bytes=VMEM_LIMIT),
        cost_estimate=pl.CostEstimate(flops=weight, bytes_accessed=weight // 100, transcendentals=0),
        name=name,
    )(*scalars, *arrays)


def slots_kernel(adapter_ref, table_ref, slots_ref):
    for request in range(slots_ref.shape[0]):
        slots_ref[request] = table_ref[adapter_ref[request]]


def slots_of(request_adapter, adapter_slot_table):
    return pl.pallas_call(
        slots_kernel,
        in_specs=[pl.BlockSpec(memory_space=pltpu.SMEM)] * 2,
        out_specs=pl.BlockSpec(memory_space=pltpu.SMEM),
        out_shape=jax.ShapeDtypeStruct(request_adapter.shape, jnp.int32),
        cost_estimate=pl.CostEstimate(flops=0, bytes_accessed=0, transcendentals=0),
        name="slots",
    )(request_adapter, adapter_slot_table)


def own_kernel(slots_ref, blocks_ref, near_ref, rest_ref):
    del slots_ref
    count = near_ref.shape[0]
    near_ref[...] = blocks_ref[:count]
    rest_ref[...] = blocks_ref[count : 2 * count]


def take(request, me, slots_ref, quarter_refs, out_ref, at, other=None):
    where = slots_ref[request] ^ me
    for k in range(4):

        @pl.when((where if other is not None else where & 3) == k)
        def _():
            out_ref[at] = quarter_refs[k][...]

    if other is not None:

        @pl.when(where >= 4)
        def _():
            out_ref[at] = other[...]


def choose_kernel(slots_ref, *refs):
    me = lax.axis_index("req")
    for apart in (1, 2, 3):
        take((me >> 1) ^ apart, me, slots_ref, refs[:4], refs[3 + apart], ...)


def assemble_kernel(slots_ref, *refs):
    me = lax.axis_index("req")
    where = slots_ref[me >> 1] ^ me
    for k in range(4):

        @pl.when(where == k)
        def _():
            refs[7][0] = refs[k][...]
            refs[7][1] = refs[4][...]

    @pl.when(where >= 4)
    def _():
        refs[7][0] = refs[5][...]
        refs[7][1] = refs[6][...]


def turn_kernel(slots_ref, *refs):
    assemble_kernel(slots_ref, *refs[:7], refs[11])
    choose_kernel(slots_ref, *refs[7:11], *refs[12:])


def rank_kernel(slots_ref, context_ref, held_ref, got_ref, rank_ref):
    me = lax.axis_index("req")
    first = (slots_ref[me >> 1] ^ me) & 3
    total = jnp.zeros(rank_ref.shape, jnp.float32)
    for k in range(4):
        panel_ref = (held_ref, got_ref)[k & 1].at[k >> 1]
        for head in range(0, GROUP, 2):
            context = context_ref[first ^ k, :, head * HEAD_SIZE : (head + 2) * HEAD_SIZE]
            panel = jnp.concatenate([panel_ref[head], panel_ref[head + 1]], axis=1)
            total += dot(context, panel, MINOR_BOTH)
    rank_ref[...] = total


def delta_kernel(slots_ref, near_ref, far_ref, *refs):
    out_ref, stage_ref, sems = refs[2:]
    me = lax.axis_index("req")
    first = (slots_ref[me >> 1] ^ me) & 3
    first = (first >> 1) | ((first & 1) << 1)
    rank = (near_ref[...] + far_ref[...]).astype(jnp.bfloat16)
    wide = stage_ref.shape[2]
    copies = []
    for k in (0, 2, 1, 3):
        panel_ref = refs[k & 1].at[k >> 1]
        panel = jnp.concatenate([panel_ref[b] for b in range(panel_ref.shape[0])], axis=1)
        stage_ref[k] = (2.0 * dot(rank, panel)).astype(jnp.bfloat16)
        columns = pl.ds(pl.multiple_of((first ^ (k >> 1) ^ ((k & 1) << 1)) * wide, HEAD_SIZE), wide)
        copy = pltpu.make_async_copy(stage_ref.at[k], out_ref.at[:, columns], sems.at[k])
        copy.start()
        copies.append(copy)
    for copy in copies:
        copy.wait()


def delta_of(slots, near, far, held, got):
    rows = near.shape[0]
    wide = held.shape[1] * held.shape[3]
    return pl.pallas_call(
        delta_kernel,
        in_specs=[pl.BlockSpec(memory_space=pltpu.SMEM)]
        + [pl.BlockSpec(memory_space=pltpu.VMEM)] * 4,
        out_specs=pl.BlockSpec(memory_space=pl.ANY),
        out_shape=jax.ShapeDtypeStruct((rows, 4 * wide), jnp.bfloat16),
        scratch_shapes=[pltpu.VMEM((4, rows, wide), jnp.bfloat16), pltpu.SemaphoreType.DMA((4,))],
        compiler_params=pltpu.CompilerParams(vmem_limit_bytes=VMEM_LIMIT),
        name="delta",
    )(slots, near, far, held, got)


def quarter_cut(blocks):
    count = blocks.shape[0] // 4
    return [blocks[k * count : (k + 1) * count] for k in range(4)]


def spread(cut):
    return cut[:1] + [swapped(cut[k], "req", k) for k in (1, 2, 3)]


def after(earlier, value):
    return lax.optimization_barrier((earlier, value))[1]


def spread_in_turn(over_x, own, earlier):
    count = own[0].shape[0]
    over_x = after(earlier, over_x)
    return [own[0], over_x[:count], swapped(own[1], "req", 2), swapped(over_x[count:], "req", 2)]


def deliver(slots, quarters, weight=0):
    shape = jax.ShapeDtypeStruct(quarters[0].shape, quarters[0].dtype)
    sent = in_vmem(choose_kernel, "choose", [shape] * 3, slots, *quarters, weight=weight)
    return sent, [swapped(panel, "req", 2 * apart) for apart, panel in enumerate(sent, 1)]


def assemble(slots, quarters, came, weight=0):
    both = jax.ShapeDtypeStruct((2, *came[0].shape), came[0].dtype)
    return in_vmem(assemble_kernel, "assemble", both, slots, *quarters, *came, weight=weight)


def eight_way(queries, keys, values, down, up, request_adapter, adapter_slot_table):
    slots = slots_of(request_adapter, adapter_slot_table)
    down_cut = quarter_cut(down)
    down_quarters = spread(down_cut)
    half = up.shape[0] // 2
    up = after(down_cut, up)
    up_half = up[half:]
    quarter = jax.ShapeDtypeStruct((half // 2, *up.shape[1:]), up.dtype)
    up_own = in_vmem(own_kernel, "own", [quarter] * 2, slots, up)
    up_over_x = swapped(up_half, "req", 1)
    down_sent, down_came = deliver(slots, down_quarters, WEIGHT)
    far = swapped(jnp.concatenate(after(down_sent, (keys, values)), axis=1), "req", 1)
    up_quarters = spread_in_turn(up_over_x, up_own, down_sent)
    both = jax.ShapeDtypeStruct((2, *down_came[0].shape), down.dtype)
    one = jax.ShapeDtypeStruct(up_quarters[0].shape, up.dtype)
    parts = (*down_quarters, *down_came, *up_quarters)
    down_held, *up_sent = in_vmem(turn_kernel, "turn", [both] + [one] * 3, slots, *parts, weight=WEIGHT)
    up_came = [swapped(panel, "req", 2 * apart) for apart, panel in enumerate(up_sent, 1)]
    down_got = swapped(down_held, "req", 1)
    context = attend(queries, keys, values, after(up_sent, far))
    up_held = assemble(slots, up_quarters, after(context, up_came), 1000_000_000)
    up_got = swapped(up_held, "req", 1)
    rank_shape = jax.ShapeDtypeStruct((context.shape[1], ADAPTER_RANK), jnp.float32)
    rank = in_vmem(rank_kernel, "rank_mix", rank_shape, slots, context, down_held, down_got)
    return delta_of(slots, rank, swapped(rank, "tp", 1), up_held, up_got)


def any_way(context, down, up, slots):
    partner_count = lax.axis_size("req")
    rows = context.shape[1]

    def exchanged(blocks):
        slot_count, block_count = blocks.shape[:2]
        tail = blocks.shape[2] // partner_count
        cut = blocks.reshape(slot_count, block_count, partner_count, tail, blocks.shape[3])
        cut = jnp.moveaxis(cut, 2, 1)
        library = lax.all_to_all(cut, "req", split_axis=1, concat_axis=0, tiled=True)[:, 0]
        wanted = jnp.take(library, slots[jnp.arange(partner_count) // 2], axis=0)
        return lax.all_to_all(wanted, "req", split_axis=0, concat_axis=0, tiled=True)

    down_all = exchanged(jnp.swapaxes(down, 2, 3))
    up_all = exchanged(jnp.swapaxes(up, 2, 3))
    flat = jnp.swapaxes(context, 0, 1).reshape(rows, down_all.shape[1], partner_count, down_all.shape[2])
    rank = jnp.einsum("thrp,rhpk->tk", flat, down_all, preferred_element_type=jnp.float32)
    rank = lax.psum(rank, "tp").astype(jnp.bfloat16)
    mixed = jnp.einsum("tk,rblk->tbrl", rank, up_all, preferred_element_type=jnp.float32)
    return (2.0 * mixed.reshape(rows, -1)).astype(jnp.bfloat16)


def body(
    projected_queries,
    projected_keys,
    projected_values,
    request_adapter,
    adapter_slot_table,
    adapter_down_factor,
    adapter_up_factor,
):
    down = jnp.swapaxes(adapter_down_factor, 2, 3)
    up = jnp.swapaxes(adapter_up_factor, 1, 2)
    spans = (projected_queries, projected_keys, projected_values)
    if lax.axis_size("req") == 8 and down.shape[0] == 1:
        return eight_way(*spans, down[0], up[0], request_adapter, adapter_slot_table)
    far = swapped(jnp.concatenate(spans[1:], axis=1), "req", 1)
    return any_way(attend(*spans, far), down, up, adapter_slot_table[request_adapter])


def solution(mesh):
    placed = (
        P(("groups", "req"), "tp"),
        P(("groups", "req"), "tp"),
        P(("groups", "req"), "tp"),
        P("groups"),
        P("groups"),
        P(("groups", "req"), "tp", None, None),
        P(("groups", "req"), None, "tp", None),
    )
    return jax.shard_map(
        body, mesh=mesh, in_specs=placed, out_specs=P(("groups", "req"), "tp"), check_vma=False
    )
```
